32 devices in a mesh: dp: 4 (over y, x), expert: 8 (over z, core).
Axes of the slice: x: 2, y: 2, z: 4, core: 2. Of those that a mesh axis runs over, the one named last changes fastest.
Arguments:
- tokens: bfloat16 [4096, 2048], P(('dp', 'expert')), may hold values from -6 to 6
- expert_ids: int32 [4096, 3], P(('dp', 'expert')), may hold values from 0 to 7, all different within a row; in each aligned block of 128 rows (0 to 127, 128 to 255, ...) at most 64 rows name the same one
- gate_level: int32 [4096, 3], P(('dp', 'expert')), may hold values from 0 to 15
- cost_bucket: int32 [64], P(('dp', 'expert')), may hold values from 0 to 7
- gate_table: float32 [8, 16], replicated, may hold values from 0.05 to 0.6
- gate_weight: bfloat16 [8, 2048, 768], P('expert', 'dp'), may hold values from -0.125 to 0.125
- up_weight: bfloat16 [8, 2048, 768], P('expert', 'dp'), may hold values from -0.125 to 0.125
- down_weight: bfloat16 [8, 2048, 768], P('expert', 'dp'), may hold values from -0.21875 to 0.21875
- out_grad: bfloat16 [4096, 2048], P(('dp', 'expert')), may hold values from -6 to 6
Outputs:
- output: bfloat16 [4096, 2048], P(('dp', 'expert'))
- token_grad: bfloat16 [4096, 2048], P(('dp', 'expert'))
- gate_grad: float32 [8, 2048, 768], P('expert', 'dp')
- up_grad: float32 [8, 2048, 768], P('expert', 'dp')
- down_grad: float32 [8, 2048, 768], P('expert', 'dp')
The draws below stay inside these ranges and needn't reach their ends.
Inputs may be any that keep to these rules, and one draw needn't show every extreme that they name: `expert_ids`: each row names 3 different experts. Among the rows of one device (aligned blocks of 128 rows) no expert is named more than 64 times, and in every draw some expert is named exactly 64 times in some block.
All inputs are finite; a program needn't handle non-finite values.
Results may differ from the reference program's by a relative error of at most 0.0085.
Values may be sent and summed in bfloat16 or wider, within the bound.
A program may use at most 128 MiB of HBM per device.

```python
import math
import jax
import jax.numpy as jnp
import numpy as np
from jax import lax

D = 2048
H = 768
TOP = 3
TOK_DEV = 128
TRAJ = 64
BUCKETS = 8
LEVELS = 16
EXPERTS = 8
CAP = 64
TOKENS = 4096
TRAJS = 64
N_DP = 4


def set_ends(array, rng, smallest, largest):
    longest = array.shape.index(max(array.shape))
    spots = []
    for shift in (0, 1):
        where = [jax.random.randint(jax.random.fold_in(rng, axis), (), 0, length) for axis, length in enumerate(array.shape)]
        where[longest] = (where[longest] + shift) % array.shape[longest]
        spots.append(tuple(where))
    return array.at[spots[0]].set(smallest).at[spots[1]].set(largest)


def block_levels(stream_key, dims, split, smallest, largest):
    loudness = 1.0
    for dim, blocks in split:
        heights = jax.random.uniform(jax.random.fold_in(jax.random.fold_in(stream_key, 6), dim), (blocks,), jnp.float32, smallest / len(split), largest / len(split))
        loudness = loudness * jnp.repeat(jnp.exp(heights), dims[dim] // blocks).reshape((-1,) + (1,) * (len(dims) - 1 - dim))
    return loudness


def deal_out(own_key, own, number, rows, number_of, top, most, slope):
    ranking = jax.random.permutation(own_key, number_of)
    heavy_load, usual = load_shares(number_of, rows * top, most, slope, True), load_shares(number_of, rows * top, most, slope, False)
    places = jnp.arange(number_of)

    def named(lengths, turn):
        used = int((lengths > 0).sum())
        fixed = max(1, used // 4)
        shifted = fixed + (places - fixed + turn * (used - fixed)) % max(1, number_of - fixed)
        return jnp.zeros((number_of,), jnp.int32).at[ranking[jnp.where(places < fixed, places, shifted)]].set(jnp.asarray(lengths, jnp.int32))

    lengths = jnp.where(number % 4 == 0, named(heavy_load, number // 4), named(usual, number - number // 4 - 1))
    mixed = jax.random.permutation(jax.random.fold_in(own, 3), number_of)
    source_of, taker = mixed[0:number_of // 2 * 2:2], mixed[1:number_of // 2 * 2:2]
    room = jnp.minimum(lengths[source_of] - 1, most - lengths[taker]) // 2
    room = jnp.where((source_of == ranking[0]) | (taker == ranking[0]) | (lengths[taker] == 0), 0, jnp.maximum(room, 0))
    shifted = jax.random.randint(jax.random.fold_in(own, 4), (number_of // 2,), 0, 1 << 20) % (room + 1)
    lengths = lengths.at[source_of].add(-shifted).at[taker].add(shifted)
    items = jnp.searchsorted(jnp.cumsum(lengths), jnp.arange(rows * top), side="right").astype(jnp.int32)
    listing = items.reshape(top, rows).T
    listing = listing[jax.random.permutation(jax.random.fold_in(own, 1), rows)]
    turn = jax.random.randint(jax.random.fold_in(own, 2), (rows, 1), 0, top)
    return jnp.take_along_axis(listing, (jnp.arange(top)[None, :] + turn) % top, axis=1)


def load_shares(count, total, bound, slope, full):
    loads = [(1 << 20) // math.isqrt(standing ** slope) + 1 for standing in range(1, count + 1)]
    largest = bound if full else min(bound, max(-(-total // count), total * loads[0] // sum(loads)))
    least = 1 if total - largest >= count - 1 else 0
    holding, surplus = [largest] + [least] * (count - 1), total - largest - least * (count - 1)
    while surplus > 0:
        movable = [i for i in range(1, count) if holding[i] < largest] or [i for i in range(1, count) if holding[i] < bound]
        whole, remaining = sum([loads[i] for i in movable]), surplus
        for i in movable:
            more = min(bound - holding[i], max(1, remaining * loads[i] // whole), surplus)
            holding[i] = holding[i] + more
            surplus = surplus - more
    return np.array(holding)


def scatter_about(stream_key, dims, width, most, split=(), held_as=jnp.bfloat16):
    array = jax.random.normal(stream_key, dims, jnp.float32) * width
    if len(split) > 0:
        array = block_levels(stream_key, dims, split, -0.22, 0.18) * array
    return jnp.clip(array, min=-most, max=most).astype(held_as)


def setup_inputs(seed: int = 0) -> dict:
    key_of = jax.random.split(jax.random.key(seed), 10)
    tokens = scatter_about(key_of[0], (TOKENS, D), 1.0, 6.0, ((0, 32),))
    expert_ids_keys = jax.random.split(jax.random.fold_in(key_of[1], 1), TOKENS // TOK_DEV)
    expert_ids_turns = jax.random.permutation(jax.random.fold_in(key_of[1], 3), TOKENS // TOK_DEV)
    expert_ids = jax.vmap(lambda own, number: deal_out(jax.random.fold_in(key_of[1], 2), own, number, TOK_DEV, EXPERTS, TOP, CAP, 2))(expert_ids_keys, expert_ids_turns).reshape((TOKENS, TOP))
    gate_level = set_ends(jax.random.randint(key_of[2], (TOKENS, TOP), 0, LEVELS), jax.random.fold_in(key_of[2], 1), 0, LEVELS - 1).astype(jnp.int32)
    cost_bucket = set_ends(jax.random.randint(key_of[3], (TRAJS,), 0, BUCKETS), jax.random.fold_in(key_of[3], 1), 0, BUCKETS - 1).astype(jnp.int32)
    gate_table = jnp.clip(jnp.exp(jax.random.uniform(key_of[4], (BUCKETS, LEVELS), jnp.float32, math.log(0.05), math.log(0.6))), 0.05, 0.6)
    gate_weight = scatter_about(key_of[5], (EXPERTS, D, H), D ** -0.5, 0.125, ((0, 8), (1, 4)))
    up_weight = scatter_about(key_of[6], (EXPERTS, D, H), D ** -0.5, 0.125, ((0, 8), (1, 4)))
    down_weight = scatter_about(key_of[7], (EXPERTS, D, H), H ** -0.5, 0.21875, ((0, 8), (1, 4)))
    out_grad = scatter_about(key_of[8], (TOKENS, D), 1.0, 6.0, ((0, 32),))
    return dict(tokens=tokens, expert_ids=expert_ids, gate_level=gate_level, cost_bucket=cost_bucket, gate_table=gate_table, gate_weight=gate_weight, up_weight=up_weight, down_weight=down_weight, out_grad=out_grad)


def reference(tokens, expert_ids, gate_level, cost_bucket, gate_table, gate_weight, up_weight, down_weight, out_grad):
    assigned = TOKENS * TOP
    blocks = TOKENS // TOK_DEV
    flat_ids = expert_ids.reshape(-1).astype(jnp.int32)
    marks_hot = (flat_ids[:, None] == jnp.arange(EXPERTS, dtype=jnp.int32)[None, :]).astype(jnp.int32)
    marks_hot = marks_hot.reshape(blocks, TOK_DEV * TOP, EXPERTS)
    earlier = jnp.cumsum(marks_hot, axis=1) - marks_hot
    slot_index = jnp.sum(earlier * marks_hot, axis=2).reshape(-1).astype(jnp.int32)
    block_index = (jnp.arange(assigned, dtype=jnp.int32) // (TOK_DEV * TOP)).astype(jnp.int32)
    slot_place = ((flat_ids * blocks + block_index) * CAP + slot_index).astype(jnp.int32)
    owner_row = jnp.full((EXPERTS * blocks * CAP,), assigned, jnp.int32).at[slot_place].set(jnp.arange(assigned, dtype=jnp.int32))
    token_of = jnp.where(owner_row < assigned, owner_row // TOP, TOKENS).astype(jnp.int32).reshape(EXPERTS, blocks * CAP)
    bucket_tok = jnp.repeat(cost_bucket, TRAJ)
    gate_values = gate_table[bucket_tok[:, None], gate_level]
    gate_padded = jnp.concatenate([gate_values.reshape(-1), jnp.zeros((1,), gate_values.dtype)])
    slot_gate = gate_padded[owner_row].reshape(EXPERTS, blocks * CAP)
    zero_row = jnp.zeros((1, D), tokens.dtype)
    tokens_padded = jnp.concatenate([tokens, zero_row], axis=0)
    grad_padded = jnp.concatenate([out_grad, zero_row.astype(out_grad.dtype)], axis=0)
    contract_last = (((1,), (1,)), ((), ()))

    def grouped(values):
        return values.reshape(N_DP, (blocks * CAP) // N_DP, values.shape[-1]).astype(jnp.float32)

    def settle(partial_value):
        return lax.optimization_barrier(partial_value.astype(jnp.bfloat16)).astype(jnp.float32).sum(axis=0)

    def per_expert(totals, inputs):
        out_acc, grad_acc = totals
        rows_of, gate_of, w_gate, w_up, w_down = inputs
        expert_rows = tokens_padded[rows_of]
        gate_act = jnp.dot(expert_rows, w_gate, preferred_element_type=jnp.float32)
        up_act = jnp.dot(expert_rows, w_up, preferred_element_type=jnp.float32)
        sigmoid_gate = jax.nn.sigmoid(gate_act)
        swish_gate = gate_act * sigmoid_gate
        hidden = (swish_gate * up_act).astype(jnp.bfloat16)
        result = lax.dot_general(hidden, w_down, contract_last, preferred_element_type=jnp.float32).astype(jnp.bfloat16)
        out_acc = out_acc.at[rows_of].add(gate_of[:, None] * result.astype(jnp.float32))
        scaled = (gate_of[:, None] * grad_padded[rows_of].astype(jnp.float32)).astype(jnp.bfloat16)
        grad_hidden = jnp.dot(scaled, w_down, preferred_element_type=jnp.float32)
        grad_gate_act = (grad_hidden * up_act * sigmoid_gate * (1.0 + gate_act * (1.0 - sigmoid_gate))).astype(jnp.bfloat16)
        grad_up_act = (grad_hidden * swish_gate).astype(jnp.bfloat16)
        grad_in = (lax.dot_general(grad_gate_act, w_gate, contract_last, preferred_element_type=jnp.float32)
                   + lax.dot_general(grad_up_act, w_up, contract_last, preferred_element_type=jnp.float32)).astype(jnp.bfloat16)
        grad_acc = grad_acc.at[rows_of].add(grad_in.astype(jnp.float32))
        gate_part = jnp.einsum("gmd,gmh->gdh", grouped(expert_rows), grouped(grad_gate_act), precision=lax.Precision.HIGHEST)
        up_part = jnp.einsum("gmd,gmh->gdh", grouped(expert_rows), grouped(grad_up_act), precision=lax.Precision.HIGHEST)
        down_part = jnp.einsum("gmd,gmh->gdh", grouped(scaled), grouped(hidden), precision=lax.Precision.HIGHEST)
        return (out_acc, grad_acc), (settle(gate_part), settle(up_part), settle(down_part))

    start_totals = (jnp.zeros((TOKENS + 1, D), jnp.float32), jnp.zeros((TOKENS + 1, D), jnp.float32))
    (out_acc, grad_acc), (gate_grad, up_grad, down_grad) = lax.scan(
        per_expert, start_totals, (token_of, slot_gate, gate_weight, up_weight, down_weight))
    return (out_acc[:TOKENS].astype(jnp.bfloat16), grad_acc[:TOKENS].astype(jnp.bfloat16),
            gate_grad, up_grad, down_grad)
```

```python
import functools

import jax
import jax.numpy as jnp
from jax import lax
from jax.experimental import pallas as pl
from jax.experimental.pallas import tpu as pltpu
from jax.sharding import PartitionSpec as P

MESH = pl.DeviceIdType.MESH


def places():
    d = lax.axis_index("dp")
    e = lax.axis_index("expert")
    x = lax.rem(d, 2)
    y = lax.div(d, 2)
    return d, e, y * 2 + (1 - x), (1 - y) * 2 + x, (1 - y) * 2 + (1 - x)


def gather_kernel(
    chips,
    wg, wu, wd, tok, grd, meta,
    og, ou, od, otok, ogrd, ometa,
    wsend, wrecv, zsend, zrecv, csend, crecv, local,
):
    d, e, dx, dy, _ = places()
    z = lax.div(e, 2)
    core = lax.rem(e, 2)
    sibling = z * 2 + 1 - core
    rows = wg.shape[1]
    half = rows // 2
    here_x, here_y = (dx, e), (dy, e)

    barrier = pltpu.get_barrier_semaphore()
    pl.semaphore_signal(barrier, inc=1, device_id=here_x, device_id_type=MESH)
    pl.semaphore_signal(barrier, inc=1, device_id=here_y, device_id_type=MESH)
    for k in range(1, 2 * chips):
        pl.semaphore_signal(
            barrier, inc=1, device_id=(d, lax.rem(e + k, 2 * chips)), device_id_type=MESH
        )
    pl.semaphore_wait(barrier, 2 * chips + 1)

    weights = ((wg, og), (wu, ou), (wd, od))
    blocks = ((tok, otok), (grd, ogrd), (meta, ometa))

    def own_half(w, h):
        return weights[w][0].at[0, pl.ds(h * half, half), :]

    def placed(w, owner, h):
        return weights[w][1].at[pl.ds(pl.multiple_of(owner * rows + h * half, half), half), :]

    def wcopy(w, kind, src, dst, device):
        return pltpu.make_async_remote_copy(
            src_ref=src, dst_ref=dst, send_sem=wsend.at[w, kind], recv_sem=wrecv.at[w, kind],
            device_id=device, device_id_type=MESH,
        )

    def wcopies(w):
        return (
            wcopy(w, 0, own_half(w, 0), placed(w, d, 0), here_x),
            wcopy(w, 1, own_half(w, 1), placed(w, d, 1), here_y),
            wcopy(w, 2, own_half(w, 1), placed(w, d, 1), here_x),
            wcopy(w, 3, own_half(w, 0), placed(w, d, 0), here_y),
            wcopy(w, 4, placed(w, dx, 0), placed(w, dx, 0), here_y),
            wcopy(w, 5, placed(w, dy, 1), placed(w, dy, 1), here_x),
        )

    def block(a, owner):
        return blocks[a][1].at[owner]

    def zcopy(a, way, s):
        step = 1 if way == 0 else -1
        owner = (z - step * s) * 2 + core
        src = blocks[a][0] if s == 0 else block(a, owner)
        return pltpu.make_async_remote_copy(
            src_ref=src, dst_ref=block(a, owner), send_sem=zsend.at[a, way, s],
            recv_sem=zrecv.at[a, way, s], device_id=(d, e + 2 * step), device_id_type=MESH,
        )

    def zhas(way, s):
        if way == 0:
            return jnp.logical_and(z < chips - 1, z >= s)
        return jnp.logical_and(z > 0, z + s < chips)

    def zgets(way, s):
        return z - 1 - s >= 0 if way == 0 else z + 1 + s < chips

    def ccopy(a, way, s):
        step = 1 if way == 0 else -1
        owner = e if s < 0 else (z - step * (s + 1)) * 2 + core
        src = blocks[a][0] if s < 0 else block(a, owner)
        k = 0 if s < 0 else 1 + way * (chips - 1) + s
        return pltpu.make_async_remote_copy(
            src_ref=src, dst_ref=block(a, owner), send_sem=csend.at[a, k],
            recv_sem=crecv.at[a, k], device_id=(d, sibling), device_id_type=MESH,
        )

    order = (2, 0, 1)
    for a in order:
        for way in (0, 1):
            @pl.when(zhas(way, 0))
            def _(a=a, way=way):
                zcopy(a, way, 0).start()
    sent = [wcopies(w) for w in range(3)]
    for w in range(3):
        for k in range(4):
            sent[w][k].start()
    for a in order:
        ccopy(a, 0, -1).start()
    here = [
        pltpu.make_async_copy(weights[w][0].at[0], weights[w][1].at[pl.ds(pl.multiple_of(d * rows, rows), rows), :], local.at[w])
        for w in range(3)
    ] + [pltpu.make_async_copy(blocks[a][0], block(a, e), local.at[3 + a]) for a in range(3)]
    for c in here:
        c.start()

    def zstep(a, s):
        for way in (0, 1):
            @pl.when(zgets(way, s))
            def _(way=way):
                zcopy(a, way, s).wait_recv()
                if s < chips - 2:
                    @pl.when(zhas(way, s + 1))
                    def _():
                        zcopy(a, way, s + 1).start()
                ccopy(a, way, s).start()

    def wstep(w):
        sent[w][0].wait_recv()
        sent[w][4].start()
        sent[w][1].wait_recv()
        sent[w][5].start()

    steps = [(s, a) for s in range(chips - 1) for a in order]
    at = 0
    for i, (s, a) in enumerate(steps):
        zstep(a, s)
        if a != 2 and at < 3:
            wstep(at)
            at += 1
    while at < 3:
        wstep(at)
        at += 1
    for c in here:
        c.wait()
    for w in range(3):
        for k in range(2, 6):
            sent[w][k].wait_recv()
        for k in range(6):
            sent[w][k].wait_send()
    for a in order:
        for s in range(-1, chips - 1):
            for way in (0, 1):
                if s < 0:
                    if way == 0:
                        ccopy(a, 0, -1).wait()
                    continue

                @pl.when(zhas(way, s))
                def _(way=way, s=s):
                    zcopy(a, way, s).wait_send()

                @pl.when(zgets(way, s))
                def _(way=way, s=s):
                    ccopy(a, way, s).wait()


def scatter_kernel(
    members,
    pg, pu, pd, res, gin,
    xg, xu, xd, yg, yu, yd, rres, rgin,
    land, part, wsend, wrecv, asend, arecv, local,
):
    d, e, dx, dy, dd = places()
    rows = xg.shape[0]
    half = rows // 2
    here_x, here_y = (dx, e), (dy, e)

    barrier = pltpu.get_barrier_semaphore()
    pl.semaphore_signal(barrier, inc=1, device_id=here_x, device_id_type=MESH)
    pl.semaphore_signal(barrier, inc=1, device_id=here_y, device_id_type=MESH)
    for k in range(1, members):
        pl.semaphore_signal(
            barrier, inc=1, device_id=(d, lax.rem(e + k, members)), device_id_type=MESH
        )
    pl.semaphore_wait(barrier, 1 + members)

    partials = (pg, pu, pd)
    from_x = (xg, xu, xd)
    from_y = (yg, yu, yd)

    def piece(w, owner, h):
        return partials[w].at[pl.ds(pl.multiple_of(owner * rows + h * half, half), half), :]

    def wcopy(w, kind, src, dst, device):
        return pltpu.make_async_remote_copy(
            src_ref=src, dst_ref=dst, send_sem=wsend.at[w, kind], recv_sem=wrecv.at[w, kind],
            device_id=device, device_id_type=MESH,
        )

    def spot(ref, h):
        return ref.at[pl.ds(h * half, half), :]

    def wcopies(w):
        return (
            wcopy(w, 0, piece(w, dd, 0), land.at[w, 0], here_x),
            wcopy(w, 1, piece(w, dd, 1), land.at[w, 1], here_y),
            wcopy(w, 2, piece(w, dx, 0), spot(from_x[w], 0), here_x),
            wcopy(w, 3, piece(w, dy, 1), spot(from_y[w], 1), here_y),
            wcopy(w, 4, part.at[w, 0], spot(from_y[w], 0), here_y),
            wcopy(w, 5, part.at[w, 1], spot(from_x[w], 1), here_x),
        )

    sent = [wcopies(w) for w in range(3)]
    moves = ((res, rres), (gin, rgin))
    far = []
    for a in (0, 1):
        src, dst = moves[a]
        for k in range(1, members):
            to = lax.rem(e + k, members)
            far.append(
                pltpu.make_async_remote_copy(
                    src_ref=src.at[to], dst_ref=dst.at[e], send_sem=asend.at[a, k],
                    recv_sem=arecv.at[a, k], device_id=(d, to), device_id_type=MESH,
                )
            )
    for w in range(3):
        sent[w][0].start()
        sent[w][1].start()
    for c in far:
        c.start()
    for w in range(3):
        sent[w][2].start()
        sent[w][3].start()
    here = [
        pltpu.make_async_copy(moves[a][0].at[e], moves[a][1].at[e], local.at[a]) for a in (0, 1)
    ]
    for c in here:
        c.start()
    tile = half // 4
    for w in range(3):
        for h, owner in ((0, dy), (1, dx)):
            sent[w][h].wait_recv()

            @pl.loop(0, 4)
            def _(i, w=w, h=h, owner=owner):
                at = pl.ds(pl.multiple_of(i * tile, tile), tile)
                mine = partials[w][
                    pl.ds(pl.multiple_of(owner * rows + h * half + i * tile, tile), tile), :
                ]
                part[w, h, at, :] = (
                    land[w, h, at, :].astype(jnp.float32) + mine.astype(jnp.float32)
                ).astype(jnp.bfloat16)

            sent[w][4 + h].start()
    for c in here:
        c.wait()
    for c in far:
        c.wait()
    for w in range(3):
        for k in range(2, 6):
            sent[w][k].wait_recv()
        for k in range(6):
            sent[w][k].wait_send()


def square_shards(
    tokens, expert_ids, gate_level, cost_bucket, gate_table,
    gate_weight, up_weight, down_weight, out_grad,
):
    n_tok, width = tokens.shape
    top_count = expert_ids.shape[1]
    members = lax.axis_size("expert")
    n_dp = lax.axis_size("dp")
    chips = members // 2
    cap = min(n_tok, 4 * n_tok * top_count // (3 * members))
    shard = gate_weight.shape[1]
    units = gate_weight.shape[2]
    f32, bf16 = jnp.float32, jnp.bfloat16
    any_spec = pl.BlockSpec(memory_space=pl.ANY)
    vmem_spec = pl.BlockSpec(memory_space=pltpu.VMEM)

    bucket_tok = jnp.repeat(cost_bucket, n_tok // cost_bucket.shape[0])
    bucket_hot = bucket_tok[:, None] == jnp.arange(gate_table.shape[0], dtype=jnp.int32)[None, :]
    table_rows = jnp.sum(jnp.where(bucket_hot[:, :, None], gate_table[None], 0.0), axis=1)
    level_hot = (
        gate_level[:, :, None] == jnp.arange(gate_table.shape[1], dtype=jnp.int32)[None, None, :]
    )
    gate_values = jnp.sum(jnp.where(level_hot, table_rows[:, None, :], 0.0), axis=2)
    chosen = expert_ids[None] == jnp.arange(members, dtype=jnp.int32)[:, None, None]
    mask = jnp.sum(chosen.astype(f32), axis=2)
    gates = jnp.sum(jnp.where(chosen, gate_values[None], 0.0), axis=2)
    meta = jnp.concatenate([gates, mask], axis=0)

    def slots(choice):
        upto = jnp.arange(n_tok)[:, None] < jnp.arange(n_tok)[None, :]
        rank = jnp.dot(choice.astype(bf16), upto.astype(bf16), preferred_element_type=f32)
        same = rank[:, None, :] == jnp.arange(cap, dtype=f32)[None, :, None]
        return jnp.logical_and(same, choice[:, None, :] > 0.5)

    sds = jax.ShapeDtypeStruct
    w_gate, w_up, w_down, all_tok, all_grd, all_meta = pl.pallas_call(
        functools.partial(gather_kernel, chips),
        out_shape=[sds((n_dp * shard, units), bf16)] * 3
        + [sds((members, n_tok, width), bf16)] * 2
        + [sds((members, 2 * members, n_tok), f32)],
        in_specs=[any_spec] * 6,
        out_specs=[any_spec] * 6,
        scratch_shapes=[
            pltpu.SemaphoreType.DMA((3, 6)),
            pltpu.SemaphoreType.DMA((3, 6)),
            pltpu.SemaphoreType.DMA((3, 2, chips - 1)),
            pltpu.SemaphoreType.DMA((3, 2, chips - 1)),
            pltpu.SemaphoreType.DMA((3, 2 * chips - 1)),
            pltpu.SemaphoreType.DMA((3, 2 * chips - 1)),
            pltpu.SemaphoreType.DMA((6,)),
        ],
        compiler_params=pltpu.CompilerParams(collective_id=0, has_side_effects=True),
    )(gate_weight, up_weight, down_weight, tokens, out_grad, meta)

    me = lax.axis_index("expert")
    my_gate = lax.dynamic_index_in_dim(all_meta, me, 1, keepdims=False)
    my_mask = lax.dynamic_index_in_dim(all_meta, members + me, 1, keepdims=False)
    pick = slots(my_mask)
    slot_gate = jnp.sum(jnp.where(pick, my_gate[:, None, :], 0.0), axis=2)
    pick = pick.astype(bf16)
    batched = (((2,), (1,)), ((0,), (0,)))
    total = members * cap
    rows = lax.dot_general(pick, all_tok, batched, preferred_element_type=f32)
    rows = rows.astype(bf16).reshape(total, width)
    grad_rows = lax.dot_general(pick, all_grd, batched, preferred_element_type=f32)
    grad_rows = (grad_rows * slot_gate[:, :, None]).astype(bf16).reshape(total, width)

    contract_last = (((1,), (1,)), ((), ()))
    contract_first = (((0,), (0,)), ((), ()))
    gate_act = jnp.dot(rows, w_gate, preferred_element_type=f32)
    up_act = jnp.dot(rows, w_up, preferred_element_type=f32)
    grad_hidden = jnp.dot(grad_rows, w_down, preferred_element_type=f32)
    sig = jax.nn.sigmoid(gate_act)
    swish = gate_act * sig
    hidden = (swish * up_act).astype(bf16)
    grad_gate = (grad_hidden * up_act * sig * (1.0 + gate_act * (1.0 - sig))).astype(bf16)
    grad_up = (grad_hidden * swish).astype(bf16)
    result = lax.dot_general(hidden, w_down, contract_last, preferred_element_type=f32)
    result = result.astype(bf16).reshape(members, cap, width)
    grad_in = lax.dot_general(
        grad_gate, w_gate, contract_last, preferred_element_type=f32
    ) + lax.dot_general(grad_up, w_up, contract_last, preferred_element_type=f32)
    grad_in = grad_in.astype(bf16).reshape(members, cap, width)
    partials = [
        lax.dot_general(a, b, contract_first, preferred_element_type=f32).astype(bf16)
        for a, b in ((rows, grad_gate), (rows, grad_up), (grad_rows, hidden))
    ]

    half = shard // 2
    back = pl.pallas_call(
        functools.partial(scatter_kernel, members),
        out_shape=[sds((shard, units), bf16)] * 6 + [sds((members, cap, width), bf16)] * 2,
        in_specs=[vmem_spec] * 3 + [any_spec] * 2,
        out_specs=[any_spec] * 8,
        scratch_shapes=[
            pltpu.VMEM((3, 2, half, units), bf16),
            pltpu.VMEM((3, 2, half, units), bf16),
            pltpu.SemaphoreType.DMA((3, 6)),
            pltpu.SemaphoreType.DMA((3, 6)),
            pltpu.SemaphoreType.DMA((2, members)),
            pltpu.SemaphoreType.DMA((2, members)),
            pltpu.SemaphoreType.DMA((2,)),
        ],
        compiler_params=pltpu.CompilerParams(
            collective_id=1, has_side_effects=True, vmem_limit_bytes=40 * 1024 * 1024
        ),
    )(*partials, result, grad_in)

    own = lax.axis_index("dp") * shard
    grads = [
        (
            lax.dynamic_slice_in_dim(partials[w], own, shard, 0).astype(f32)
            + back[w].astype(f32)
            + back[3 + w].astype(f32)
        )[None]
        for w in range(3)
    ]
    place = slots(mask)
    weight = jnp.where(place, gates[:, None, :], 0.0).reshape(total, n_tok)
    high = weight.astype(bf16)
    low = (weight - high.astype(f32)).astype(bf16)
    returned = back[6].reshape(total, width)
    output = lax.dot_general(
        jnp.concatenate([high, low], axis=1), returned, contract_first, preferred_element_type=f32
    )
    output = (output[:n_tok] + output[n_tok:]).astype(bf16)
    token_grad = lax.dot_general(
        place.reshape(total, n_tok).astype(bf16),
        back[7].reshape(total, width),
        contract_first,
        preferred_element_type=f32,
    ).astype(bf16)
    return (output, token_grad, *grads)


def move_rows(buffer):
    return lax.all_to_all(buffer, "expert", split_axis=0, concat_axis=0, tiled=True)


def shards(
    tokens,
    expert_ids,
    gate_level,
    cost_bucket,
    gate_table,
    gate_weight,
    up_weight,
    down_weight,
    out_grad,
):
    local_tokens = tokens.shape[0]
    top_count = expert_ids.shape[1]
    model_width = tokens.shape[1]
    members = lax.axis_size("expert")
    capacity = min(local_tokens, 4 * local_tokens * top_count // (3 * members))
    slot_total = members * capacity
    pair_total = local_tokens * top_count
    contract_last = (((1,), (1,)), ((), ()))
    contract_first = (((0,), (0,)), ((), ()))
    gathered = (
        lax.all_gather(gate_weight, "dp", axis=1, tiled=True),
        lax.all_gather(up_weight, "dp", axis=1, tiled=True),
        lax.all_gather(down_weight, "dp", axis=1, tiled=True),
    )
    w_gate = gathered[0][0]
    w_up = gathered[1][0]
    w_down = gathered[2][0]
    flat_ids = expert_ids.reshape(-1)
    marks_hot = (flat_ids[:, None] == jnp.arange(members, dtype=jnp.int32)[None, :]).astype(
        jnp.int32
    )
    before = jnp.arange(pair_total)[:, None] > jnp.arange(pair_total)[None, :]
    earlier = jnp.dot(
        before.astype(jnp.bfloat16),
        marks_hot.astype(jnp.bfloat16),
        preferred_element_type=jnp.float32,
    ).astype(jnp.int32)
    slot_index = jnp.sum(earlier * marks_hot, axis=1)
    slot_place = flat_ids * capacity + slot_index
    owner_row = (
        jnp.full((slot_total,), pair_total, jnp.int32)
        .at[slot_place]
        .set(jnp.arange(pair_total, dtype=jnp.int32))
    )
    filled = owner_row < pair_total
    source_token = jnp.where(filled, owner_row // top_count, local_tokens)
    bucket_tok = jnp.repeat(cost_bucket, local_tokens // cost_bucket.shape[0])
    bucket_hot = (
        bucket_tok[:, None] == jnp.arange(gate_table.shape[0], dtype=jnp.int32)[None, :]
    ).astype(jnp.float32)
    table_rows = jnp.dot(bucket_hot, gate_table, precision=lax.Precision.HIGHEST)
    level_hot = (
        gate_level[:, :, None] == jnp.arange(gate_table.shape[1], dtype=jnp.int32)[None, None, :]
    ).astype(jnp.float32)
    gate_values = jnp.sum(level_hot * table_rows[:, None, :], axis=2)
    gate_padded = jnp.concatenate([gate_values.reshape(-1), jnp.zeros((1,), jnp.float32)])
    slot_gate = gate_padded[owner_row]
    zero_row = jnp.zeros((1, model_width), jnp.bfloat16)
    tokens_padded = jnp.concatenate([tokens, zero_row], axis=0)
    send_rows = tokens_padded[source_token].reshape(members, capacity, model_width)
    expert_rows = move_rows(send_rows).reshape(slot_total, model_width)
    gate_act = jnp.dot(expert_rows, w_gate, preferred_element_type=jnp.float32)
    up_act = jnp.dot(expert_rows, w_up, preferred_element_type=jnp.float32)
    sigmoid_gate = jax.nn.sigmoid(gate_act)
    swish_gate = gate_act * sigmoid_gate
    hidden = (swish_gate * up_act).astype(jnp.bfloat16)
    result = lax.dot_general(
        hidden, w_down, contract_last, preferred_element_type=jnp.float32
    ).astype(jnp.bfloat16)
    returned_rows = move_rows(result.reshape(members, capacity, model_width)).reshape(
        slot_total, model_width
    )
    picked = (
        returned_rows[slot_place].reshape(local_tokens, top_count, model_width).astype(jnp.float32)
    )
    output = jnp.sum(picked * gate_values[:, :, None], axis=1).astype(jnp.bfloat16)
    grad_padded = jnp.concatenate([out_grad, zero_row], axis=0)
    scaled = (grad_padded[source_token].astype(jnp.float32) * slot_gate[:, None]).astype(
        jnp.bfloat16
    )
    grad_rows = move_rows(scaled.reshape(members, capacity, model_width)).reshape(
        slot_total, model_width
    )
    grad_hidden = jnp.dot(grad_rows, w_down, preferred_element_type=jnp.float32)
    grad_gate_act = (
        grad_hidden * up_act * sigmoid_gate * (1.0 + gate_act * (1.0 - sigmoid_gate))
    ).astype(jnp.bfloat16)
    grad_up_act = (grad_hidden * swish_gate).astype(jnp.bfloat16)
    grad_in = (
        lax.dot_general(grad_gate_act, w_gate, contract_last, preferred_element_type=jnp.float32)
        + lax.dot_general(grad_up_act, w_up, contract_last, preferred_element_type=jnp.float32)
    ).astype(jnp.bfloat16)
    grad_back = move_rows(grad_in.reshape(members, capacity, model_width)).reshape(
        slot_total, model_width
    )
    token_grad = jnp.sum(
        grad_back[slot_place].reshape(local_tokens, top_count, model_width).astype(jnp.float32),
        axis=1,
    ).astype(jnp.bfloat16)
    both_act = jnp.concatenate([grad_gate_act, grad_up_act], axis=1)
    hidden_units = w_gate.shape[1]
    first_part = lax.dot_general(
        expert_rows, both_act, contract_first, preferred_element_type=jnp.float32
    )
    second_part = lax.dot_general(
        grad_rows, hidden, contract_first, preferred_element_type=jnp.float32
    )
    weight_sums = lax.psum_scatter(
        jnp.concatenate([first_part, second_part], axis=1).astype(jnp.bfloat16),
        "dp",
        scatter_dimension=0,
        tiled=True,
    ).astype(jnp.float32)
    gate_grad = weight_sums[:, :hidden_units][None]
    up_grad = weight_sums[:, hidden_units : 2 * hidden_units][None]
    down_grad = weight_sums[:, 2 * hidden_units :][None]
    return (output, token_grad, gate_grad, up_grad, down_grad)


def solution(mesh):
    members = mesh.shape["expert"]
    square = mesh.shape["dp"] == 4 and members % 2 == 0 and 4 <= members <= 16

    return jax.shard_map(
        square_shards if square else shards,
        mesh=mesh,
        in_specs=(
            P(("dp", "expert"), None),
            P(("dp", "expert"), None),
            P(("dp", "expert"), None),
            P(("dp", "expert")),
            P(),
            P("expert", "dp", None),
            P("expert", "dp", None),
            P("expert", "dp", None),
            P(("dp", "expert"), None),
        ),
        out_specs=(
            P(("dp", "expert"), None),
            P(("dp", "expert"), None),
            P("expert", "dp", None),
            P("expert", "dp", None),
            P("expert", "dp", None),
        ),
        check_vma=False,
    )
```

```python
import functools

import jax
import jax.numpy as jnp
from jax import lax
from jax.experimental import pallas as pl
from jax.experimental.pallas import tpu as pltpu
from jax.sharding import PartitionSpec as P

MESH = pl.DeviceIdType.MESH


def places():
    d = lax.axis_index("dp")
    e = lax.axis_index("expert")
    x = lax.rem(d, 2)
    y = lax.div(d, 2)
    return d, e, y * 2 + (1 - x), (1 - y) * 2 + x, (1 - y) * 2 + (1 - x)


def gather_kernel(
    chips,
    wg, wu, wd, tok, grd, meta,
    og, ou, od, otok, ogrd, ometa,
    wsend, wrecv, zsend, zrecv, csend, crecv, local,
):
    d, e, dx, dy, _ = places()
    z = lax.div(e, 2)
    core = lax.rem(e, 2)
    sibling = z * 2 + 1 - core
    rows = wg.shape[1]
    half = rows // 2
    here_x, here_y = (dx, e), (dy, e)

    barrier = pltpu.get_barrier_semaphore()
    pl.semaphore_signal(barrier, inc=1, device_id=here_x, device_id_type=MESH)
    pl.semaphore_signal(barrier, inc=1, device_id=here_y, device_id_type=MESH)
    for k in range(1, 2 * chips):
        pl.semaphore_signal(
            barrier, inc=1, device_id=(d, lax.rem(e + k, 2 * chips)), device_id_type=MESH
        )
    pl.semaphore_wait(barrier, 2 * chips + 1)

    weights = ((wg, og), (wu, ou), (wd, od))
    blocks = ((tok, otok), (grd, ogrd), (meta, ometa))

    def own_half(w, h):
        return weights[w][0].at[0, pl.ds(h * half, half), :]

    def placed(w, owner, h):
        return weights[w][1].at[pl.ds(pl.multiple_of(owner * rows + h * half, half), half), :]

    def wcopy(w, kind, src, dst, device):
        return pltpu.make_async_remote_copy(
            src_ref=src, dst_ref=dst, send_sem=wsend.at[w, kind], recv_sem=wrecv.at[w, kind],
            device_id=device, device_id_type=MESH,
        )

    def wcopies(w):
        return (
            wcopy(w, 0, own_half(w, 0), placed(w, d, 0), here_x),
            wcopy(w, 1, own_half(w, 1), placed(w, d, 1), here_y),
            wcopy(w, 2, own_half(w, 1), placed(w, d, 1), here_x),
            wcopy(w, 3, own_half(w, 0), placed(w, d, 0), here_y),
            wcopy(w, 4, placed(w, dx, 0), placed(w, dx, 0), here_y),
            wcopy(w, 5, placed(w, dy, 1), placed(w, dy, 1), here_x),
        )

    def block(a, owner):
        return blocks[a][1].at[owner]

    def zcopy(a, way, s):
        step = 1 if way == 0 else -1
        owner = (z - step * s) * 2 + core
        src = blocks[a][0] if s == 0 else block(a, owner)
        return pltpu.make_async_remote_copy(
            src_ref=src, dst_ref=block(a, owner), send_sem=zsend.at[a, way, s],
            recv_sem=zrecv.at[a, way, s], device_id=(d, e + 2 * step), device_id_type=MESH,
        )

    def zhas(way, s):
        if way == 0:
            return jnp.logical_and(z < chips - 1, z >= s)
        return jnp.logical_and(z > 0, z + s < chips)

    def zgets(way, s):
        return z - 1 - s >= 0 if way == 0 else z + 1 + s < chips

    def ccopy(a, way, s):
        step = 1 if way == 0 else -1
        owner = e if s < 0 else (z - step * (s + 1)) * 2 + core
        src = blocks[a][0] if s < 0 else block(a, owner)
        k = 0 if s < 0 else 1 + way * (chips - 1) + s
        return pltpu.make_async_remote_copy(
            src_ref=src, dst_ref=block(a, owner), send_sem=csend.at[a, k],
            recv_sem=crecv.at[a, k], device_id=(d, sibling), device_id_type=MESH,
        )

    order = (2, 0, 1)
    for a in order:
        for way in (0, 1):
            @pl.when(zhas(way, 0))
            def _(a=a, way=way):
                zcopy(a, way, 0).start()
    sent = [wcopies(w) for w in range(3)]
    for w in range(3):
        sent[w][0].start()
        sent[w][1].start()
    sent[0][2].start()
    sent[0][3].start()
    for a in order:
        ccopy(a, 0, -1).start()
    here = [
        pltpu.make_async_copy(weights[w][0].at[0], weights[w][1].at[pl.ds(pl.multiple_of(d * rows, rows), rows), :], local.at[w])
        for w in range(3)
    ] + [pltpu.make_async_copy(blocks[a][0], block(a, e), local.at[3 + a]) for a in range(3)]
    for c in here:
        c.start()

    def zstep(a, s):
        for way in (0, 1):
            @pl.when(zgets(way, s))
            def _(way=way):
                zcopy(a, way, s).wait_recv()
                if s < chips - 2:
                    @pl.when(zhas(way, s + 1))
                    def _():
                        zcopy(a, way, s + 1).start()
                ccopy(a, way, s).start()

    def wstep(w):
        sent[w][0].wait_recv()
        sent[w][4].start()
        sent[w][1].wait_recv()
        sent[w][5].start()
        if w > 0:
            sent[w][2].start()
            sent[w][3].start()

    for i in range(chips - 1):
        for a in order:
            zstep(a, i)
        if i == 0:
            for w in range(3):
                wstep(w)
    for c in here:
        c.wait()
    for w in range(3):
        for k in range(2, 6):
            sent[w][k].wait_recv()
        for k in range(6):
            sent[w][k].wait_send()
    for a in order:
        for s in range(-1, chips - 1):
            for way in (0, 1):
                if s < 0:
                    if way == 0:
                        ccopy(a, 0, -1).wait()
                    continue

                @pl.when(zhas(way, s))
                def _(way=way, s=s):
                    zcopy(a, way, s).wait_send()

                @pl.when(zgets(way, s))
                def _(way=way, s=s):
                    ccopy(a, way, s).wait()


def scatter_kernel(
    members,
    rows_ref, grad_ref, gg, gu, hid, res, gin,
    xg, xu, xd, yg, yu, yd, rres, rgin, mg, mu, md,
    pieces, land, part, wsend, wrecv, asend, arecv, local,
):
    d, e, dx, dy, dd = places()
    rows = xg.shape[0]
    half = rows // 2
    here_x, here_y = (dx, e), (dy, e)

    barrier = pltpu.get_barrier_semaphore()
    pl.semaphore_signal(barrier, inc=1, device_id=here_x, device_id_type=MESH)
    pl.semaphore_signal(barrier, inc=1, device_id=here_y, device_id_type=MESH)
    for k in range(1, members):
        pl.semaphore_signal(
            barrier, inc=1, device_id=(d, lax.rem(e + k, members)), device_id_type=MESH
        )
    pl.semaphore_wait(barrier, 1 + members)

    factors = ((rows_ref, gg), (rows_ref, gu), (grad_ref, hid))
    mine = (mg, mu, md)
    from_x = (xg, xu, xd)
    from_y = (yg, yu, yd)

    def product(w, owner, h):
        left, right = factors[w]
        columns = pl.ds(pl.multiple_of(owner * rows + h * half, half), half)
        return lax.dot_general(
            left[:, columns], right[...], (((0,), (0,)), ((), ())),
            preferred_element_type=jnp.float32,
        ).astype(jnp.bfloat16)

    def wcopy(w, kind, src, dst, device):
        return pltpu.make_async_remote_copy(
            src_ref=src, dst_ref=dst, send_sem=wsend.at[w, kind], recv_sem=wrecv.at[w, kind],
            device_id=device, device_id_type=MESH,
        )

    def spot(ref, h):
        return ref.at[pl.ds(h * half, half), :]

    def wcopies(w):
        return (
            wcopy(w, 0, pieces.at[w, 0, 0], land.at[w, 0], here_x),
            wcopy(w, 1, pieces.at[w, 0, 1], land.at[w, 1], here_y),
            wcopy(w, 2, pieces.at[w, 1, 0], spot(from_x[w], 0), here_x),
            wcopy(w, 3, pieces.at[w, 2, 1], spot(from_y[w], 1), here_y),
            wcopy(w, 4, part.at[w, 0], spot(from_y[w], 0), here_y),
            wcopy(w, 5, part.at[w, 1], spot(from_x[w], 1), here_x),
        )

    sent = [wcopies(w) for w in range(3)]
    moves = ((res, rres), (gin, rgin))
    far = []
    for a in (0, 1):
        src, dst = moves[a]
        for k in range(1, members):
            to = lax.rem(e + k, members)
            far.append(
                pltpu.make_async_remote_copy(
                    src_ref=src.at[to], dst_ref=dst.at[e], send_sem=asend.at[a, k],
                    recv_sem=arecv.at[a, k], device_id=(d, to), device_id_type=MESH,
                )
            )
    for c in far:
        c.start()
    here = [
        pltpu.make_async_copy(moves[a][0].at[e], moves[a][1].at[e], local.at[a]) for a in (0, 1)
    ]
    for c in here:
        c.start()
    for w in range(3):
        for h in (0, 1):
            pieces[w, 0, h] = product(w, dd, h)
            sent[w][h].start()
    for w in range(3):
        pieces[w, 1, 0] = product(w, dx, 0)
        sent[w][2].start()
        pieces[w, 2, 1] = product(w, dy, 1)
        sent[w][3].start()
    for w in range(3):
        pieces[w, 2, 0] = product(w, dy, 0)
        pieces[w, 1, 1] = product(w, dx, 1)
    for w in range(3):
        for h in (0, 1):
            mine[w][pl.ds(h * half, half), :] = product(w, d, h)
    tile = half // 4
    for w in range(3):
        for h, slot in ((0, 2), (1, 1)):
            sent[w][h].wait_recv()

            @pl.loop(0, 4)
            def _(i, w=w, h=h, slot=slot):
                at = pl.ds(pl.multiple_of(i * tile, tile), tile)
                part[w, h, at, :] = (
                    land[w, h, at, :].astype(jnp.float32)
                    + pieces[w, slot, h, at, :].astype(jnp.float32)
                ).astype(jnp.bfloat16)

            sent[w][4 + h].start()
    for c in here:
        c.wait()
    for c in far:
        c.wait()
    for w in range(3):
        for k in range(2, 6):
            sent[w][k].wait_recv()
        for k in range(6):
            sent[w][k].wait_send()


def square_shards(
    tokens, expert_ids, gate_level, cost_bucket, gate_table,
    gate_weight, up_weight, down_weight, out_grad,
):
    n_tok, width = tokens.shape
    top_count = expert_ids.shape[1]
    members = lax.axis_size("expert")
    n_dp = lax.axis_size("dp")
    chips = members // 2
    cap = min(n_tok, 4 * n_tok * top_count // (3 * members))
    shard = gate_weight.shape[1]
    units = gate_weight.shape[2]
    f32, bf16 = jnp.float32, jnp.bfloat16
    any_spec = pl.BlockSpec(memory_space=pl.ANY)
    vmem_spec = pl.BlockSpec(memory_space=pltpu.VMEM)

    bucket_tok = jnp.repeat(cost_bucket, n_tok // cost_bucket.shape[0])
    bucket_hot = bucket_tok[:, None] == jnp.arange(gate_table.shape[0], dtype=jnp.int32)[None, :]
    table_rows = jnp.sum(jnp.where(bucket_hot[:, :, None], gate_table[None], 0.0), axis=1)
    level_hot = (
        gate_level[:, :, None] == jnp.arange(gate_table.shape[1], dtype=jnp.int32)[None, None, :]
    )
    gate_values = jnp.sum(jnp.where(level_hot, table_rows[:, None, :], 0.0), axis=2)
    chosen = expert_ids[None] == jnp.arange(members, dtype=jnp.int32)[:, None, None]
    mask = jnp.sum(chosen.astype(f32), axis=2)
    gates = jnp.sum(jnp.where(chosen, gate_values[None], 0.0), axis=2)
    meta = jnp.concatenate([gates, mask], axis=0)

    def slots(choice):
        upto = jnp.arange(n_tok)[:, None] < jnp.arange(n_tok)[None, :]
        rank = jnp.dot(choice.astype(bf16), upto.astype(bf16), preferred_element_type=f32)
        same = rank[:, None, :] == jnp.arange(cap, dtype=f32)[None, :, None]
        return jnp.logical_and(same, choice[:, None, :] > 0.5)

    sds = jax.ShapeDtypeStruct
    w_gate, w_up, w_down, all_tok, all_grd, all_meta = pl.pallas_call(
        functools.partial(gather_kernel, chips),
        out_shape=[sds((n_dp * shard, units), bf16)] * 3
        + [sds((members, n_tok, width), bf16)] * 2
        + [sds((members, 2 * members, n_tok), f32)],
        in_specs=[any_spec] * 6,
        out_specs=[any_spec] * 6,
        scratch_shapes=[
            pltpu.SemaphoreType.DMA((3, 6)),
            pltpu.SemaphoreType.DMA((3, 6)),
            pltpu.SemaphoreType.DMA((3, 2, chips - 1)),
            pltpu.SemaphoreType.DMA((3, 2, chips - 1)),
            pltpu.SemaphoreType.DMA((3, 2 * chips - 1)),
            pltpu.SemaphoreType.DMA((3, 2 * chips - 1)),
            pltpu.SemaphoreType.DMA((6,)),
        ],
        compiler_params=pltpu.CompilerParams(collective_id=0, has_side_effects=True),
    )(gate_weight, up_weight, down_weight, tokens, out_grad, meta)

    me = lax.axis_index("expert")
    my_gate = lax.dynamic_index_in_dim(all_meta, me, 1, keepdims=False)
    my_mask = lax.dynamic_index_in_dim(all_meta, members + me, 1, keepdims=False)
    pick = slots(my_mask)
    slot_gate = jnp.sum(jnp.where(pick, my_gate[:, None, :], 0.0), axis=2)
    pick = pick.astype(bf16)
    batched = (((2,), (1,)), ((0,), (0,)))
    total = members * cap
    rows = lax.dot_general(pick, all_tok, batched, preferred_element_type=f32)
    rows = rows.astype(bf16).reshape(total, width)
    grad_rows = lax.dot_general(pick, all_grd, batched, preferred_element_type=f32)
    grad_rows = (grad_rows * slot_gate[:, :, None]).astype(bf16).reshape(total, width)

    contract_last = (((1,), (1,)), ((), ()))
    contract_first = (((0,), (0,)), ((), ()))
    gate_act = jnp.dot(rows, w_gate, preferred_element_type=f32)
    up_act = jnp.dot(rows, w_up, preferred_element_type=f32)
    grad_hidden = jnp.dot(grad_rows, w_down, preferred_element_type=f32)
    sig = jax.nn.sigmoid(gate_act)
    swish = gate_act * sig
    hidden = (swish * up_act).astype(bf16)
    grad_gate = (grad_hidden * up_act * sig * (1.0 + gate_act * (1.0 - sig))).astype(bf16)
    grad_up = (grad_hidden * swish).astype(bf16)
    result = lax.dot_general(hidden, w_down, contract_last, preferred_element_type=f32)
    result = result.astype(bf16).reshape(members, cap, width)
    grad_in = lax.dot_general(
        grad_gate, w_gate, contract_last, preferred_element_type=f32
    ) + lax.dot_general(grad_up, w_up, contract_last, preferred_element_type=f32)
    grad_in = grad_in.astype(bf16).reshape(members, cap, width)
    half = shard // 2
    back = pl.pallas_call(
        functools.partial(scatter_kernel, members),
        out_shape=[sds((shard, units), bf16)] * 6 + [sds((members, cap, width), bf16)] * 2
        + [sds((shard, units), bf16)] * 3,
        in_specs=[vmem_spec] * 5 + [any_spec] * 2,
        out_specs=[any_spec] * 8 + [vmem_spec] * 3,
        scratch_shapes=[
            pltpu.VMEM((3, 3, 2, half, units), bf16),
            pltpu.VMEM((3, 2, half, units), bf16),
            pltpu.VMEM((3, 2, half, units), bf16),
            pltpu.SemaphoreType.DMA((3, 6)),
            pltpu.SemaphoreType.DMA((3, 6)),
            pltpu.SemaphoreType.DMA((2, members)),
            pltpu.SemaphoreType.DMA((2, members)),
            pltpu.SemaphoreType.DMA((2,)),
        ],
        compiler_params=pltpu.CompilerParams(
            collective_id=1, has_side_effects=True, vmem_limit_bytes=40 * 1024 * 1024
        ),
    )(rows, grad_rows, grad_gate, grad_up, hidden, result, grad_in)

    grads = [
        (
            back[8 + w].astype(f32)
            + back[w].astype(f32)
            + back[3 + w].astype(f32)
        )[None]
        for w in range(3)
    ]
    place = slots(mask)
    weight = jnp.where(place, gates[:, None, :], 0.0).reshape(total, n_tok)
    high = weight.astype(bf16)
    low = (weight - high.astype(f32)).astype(bf16)
    returned = back[6].reshape(total, width)
    output = lax.dot_general(
        jnp.concatenate([high, low], axis=1), returned, contract_first, preferred_element_type=f32
    )
    output = (output[:n_tok] + output[n_tok:]).astype(bf16)
    token_grad = lax.dot_general(
        place.reshape(total, n_tok).astype(bf16),
        back[7].reshape(total, width),
        contract_first,
        preferred_element_type=f32,
    ).astype(bf16)
    return (output, token_grad, *grads)


def move_rows(buffer):
    return lax.all_to_all(buffer, "expert", split_axis=0, concat_axis=0, tiled=True)


def shards(
    tokens,
    expert_ids,
    gate_level,
    cost_bucket,
    gate_table,
    gate_weight,
    up_weight,
    down_weight,
    out_grad,
):
    local_tokens = tokens.shape[0]
    top_count = expert_ids.shape[1]
    model_width = tokens.shape[1]
    members = lax.axis_size("expert")
    capacity = min(local_tokens, 4 * local_tokens * top_count // (3 * members))
    slot_total = members * capacity
    pair_total = local_tokens * top_count
    contract_last = (((1,), (1,)), ((), ()))
    contract_first = (((0,), (0,)), ((), ()))
    gathered = (
        lax.all_gather(gate_weight, "dp", axis=1, tiled=True),
        lax.all_gather(up_weight, "dp", axis=1, tiled=True),
        lax.all_gather(down_weight, "dp", axis=1, tiled=True),
    )
    w_gate = gathered[0][0]
    w_up = gathered[1][0]
    w_down = gathered[2][0]
    flat_ids = expert_ids.reshape(-1)
    marks_hot = (flat_ids[:, None] == jnp.arange(members, dtype=jnp.int32)[None, :]).astype(
        jnp.int32
    )
    before = jnp.arange(pair_total)[:, None] > jnp.arange(pair_total)[None, :]
    earlier = jnp.dot(
        before.astype(jnp.bfloat16),
        marks_hot.astype(jnp.bfloat16),
        preferred_element_type=jnp.float32,
    ).astype(jnp.int32)
    slot_index = jnp.sum(earlier * marks_hot, axis=1)
    slot_place = flat_ids * capacity + slot_index
    owner_row = (
        jnp.full((slot_total,), pair_total, jnp.int32)
        .at[slot_place]
        .set(jnp.arange(pair_total, dtype=jnp.int32))
    )
    filled = owner_row < pair_total
    source_token = jnp.where(filled, owner_row // top_count, local_tokens)
    bucket_tok = jnp.repeat(cost_bucket, local_tokens // cost_bucket.shape[0])
    bucket_hot = (
        bucket_tok[:, None] == jnp.arange(gate_table.shape[0], dtype=jnp.int32)[None, :]
    ).astype(jnp.float32)
    table_rows = jnp.dot(bucket_hot, gate_table, precision=lax.Precision.HIGHEST)
    level_hot = (
        gate_level[:, :, None] == jnp.arange(gate_table.shape[1], dtype=jnp.int32)[None, None, :]
    ).astype(jnp.float32)
    gate_values = jnp.sum(level_hot * table_rows[:, None, :], axis=2)
    gate_padded = jnp.concatenate([gate_values.reshape(-1), jnp.zeros((1,), jnp.float32)])
    slot_gate = gate_padded[owner_row]
    zero_row = jnp.zeros((1, model_width), jnp.bfloat16)
    tokens_padded = jnp.concatenate([tokens, zero_row], axis=0)
    send_rows = tokens_padded[source_token].reshape(members, capacity, model_width)
    expert_rows = move_rows(send_rows).reshape(slot_total, model_width)
    gate_act = jnp.dot(expert_rows, w_gate, preferred_element_type=jnp.float32)
    up_act = jnp.dot(expert_rows, w_up, preferred_element_type=jnp.float32)
    sigmoid_gate = jax.nn.sigmoid(gate_act)
    swish_gate = gate_act * sigmoid_gate
    hidden = (swish_gate * up_act).astype(jnp.bfloat16)
    result = lax.dot_general(
        hidden, w_down, contract_last, preferred_element_type=jnp.float32
    ).astype(jnp.bfloat16)
    returned_rows = move_rows(result.reshape(members, capacity, model_width)).reshape(
        slot_total, model_width
    )
    picked = (
        returned_rows[slot_place].reshape(local_tokens, top_count, model_width).astype(jnp.float32)
    )
    output = jnp.sum(picked * gate_values[:, :, None], axis=1).astype(jnp.bfloat16)
    grad_padded = jnp.concatenate([out_grad, zero_row], axis=0)
    scaled = (grad_padded[source_token].astype(jnp.float32) * slot_gate[:, None]).astype(
        jnp.bfloat16
    )
    grad_rows = move_rows(scaled.reshape(members, capacity, model_width)).reshape(
        slot_total, model_width
    )
    grad_hidden = jnp.dot(grad_rows, w_down, preferred_element_type=jnp.float32)
    grad_gate_act = (
        grad_hidden * up_act * sigmoid_gate * (1.0 + gate_act * (1.0 - sigmoid_gate))
    ).astype(jnp.bfloat16)
    grad_up_act = (grad_hidden * swish_gate).astype(jnp.bfloat16)
    grad_in = (
        lax.dot_general(grad_gate_act, w_gate, contract_last, preferred_element_type=jnp.float32)
        + lax.dot_general(grad_up_act, w_up, contract_last, preferred_element_type=jnp.float32)
    ).astype(jnp.bfloat16)
    grad_back = move_rows(grad_in.reshape(members, capacity, model_width)).reshape(
        slot_total, model_width
    )
    token_grad = jnp.sum(
        grad_back[slot_place].reshape(local_tokens, top_count, model_width).astype(jnp.float32),
        axis=1,
    ).astype(jnp.bfloat16)
    both_act = jnp.concatenate([grad_gate_act, grad_up_act], axis=1)
    hidden_units = w_gate.shape[1]
    first_part = lax.dot_general(
        expert_rows, both_act, contract_first, preferred_element_type=jnp.float32
    )
    second_part = lax.dot_general(
        grad_rows, hidden, contract_first, preferred_element_type=jnp.float32
    )
    weight_sums = lax.psum_scatter(
        jnp.concatenate([first_part, second_part], axis=1).astype(jnp.bfloat16),
        "dp",
        scatter_dimension=0,
        tiled=True,
    ).astype(jnp.float32)
    gate_grad = weight_sums[:, :hidden_units][None]
    up_grad = weight_sums[:, hidden_units : 2 * hidden_units][None]
    down_grad = weight_sums[:, 2 * hidden_units :][None]
    return (output, token_grad, gate_grad, up_grad, down_grad)


def solution(mesh):
    members = mesh.shape["expert"]
    square = mesh.shape["dp"] == 4 and members % 2 == 0 and 4 <= members <= 16

    return jax.shard_map(
        square_shards if square else shards,
        mesh=mesh,
        in_specs=(
            P(("dp", "expert"), None),
            P(("dp", "expert"), None),
            P(("dp", "expert"), None),
            P(("dp", "expert")),
            P(),
            P("expert", "dp", None),
            P("expert", "dp", None),
            P("expert", "dp", None),
            P(("dp", "expert"), None),
        ),
        out_specs=(
            P(("dp", "expert"), None),
            P(("dp", "expert"), None),
            P("expert", "dp", None),
            P("expert", "dp", None),
            P("expert", "dp", None),
        ),
        check_vma=False,
    )
```
